256 devices in a mesh: leaf: 128 (over z, x, y), sub: 2 (over core).
Axes of the slice: x: 4, y: 4, z: 8, core: 2. Of those that a mesh axis runs over, the one named last changes fastest.
Arguments:
- probes: float32 [64, 262144], P(None, ('leaf', 'sub')), may hold values from -600 to 600
- points: float32 [3, 262144], P(None, ('leaf', 'sub')), may hold values from -22 to 22
- leaf_order: int32 [262144], P(('leaf', 'sub')), may hold values from 0 to 1023, as said below
- near_list: int32 [512, 4], P(('leaf', 'sub')), may hold values from 0 to 511, as said below
- far_leaf_list: int32 [512, 2], P(('leaf', 'sub')), may hold values from 0 to 511, as said below
- far_chip_list: int32 [128, 8], P('leaf'), may hold values from -1 to 127, as said below
- leaf_basis: float32 [512, 512, 256], P(('leaf', 'sub')), may hold values from -0.25 to 0.25
- transfer: float32 [512, 256, 256], P(('leaf', 'sub')), may hold values from -0.1875 to 0.1875
- far_leaf_blocks: float32 [1024, 256, 256], P(('leaf', 'sub')), may hold values from -0.25 to 0.25
- far_chip_blocks: float32 [1024, 256, 256], P('leaf'), may hold values from -0.125 to 0.125
Outputs:
- result: float32 [64, 262144], P(None, ('leaf', 'sub'))
The draws below stay inside these ranges and needn't reach their ends.
Inputs may be any that keep to these rules, and one draw needn't show every extreme that they name: `leaf_order`: each device's block of 1024 consecutive entries is a permutation of 0 to 1023. `near_list`: row l lists 4 distinct leaves, l among them, all held by the devices l // 2 - 1 to l // 2 + 1 of the joined axis leaf+sub, counted around the cycle. `far_leaf_list`: row l lists the 2 leaves of those same three devices that row l of near_list leaves out. `far_chip_list`: row k lists distinct chip clusters at cycle distance 2 to 5 from k, one to 8 of them, the used entries first and -1 in the rest; some row uses all 8.
All inputs are finite; a program needn't handle non-finite values.
Results may differ from the reference program's by a relative error of at most 0.0003.
Values sent between devices are 32-bit elements; how exact they have to be, the bound alone decides.
A program may use at most 64 MiB of HBM per device.

```python
import math
import jax
import jax.numpy as jnp
from jax import lax

LEAF = 512
RANK = 256
COLS = 64
LD = 2
CHIP_SPAN = 4
NEAR = 4
FARL = 2
FARC = 8
PTS_DEV = 1024
LEAVES = 512
CHIPS = 128
CHIP_LEAVES = 4
POINTS = 262144
DEVICES = 256


def point_layout(key):
    sub_key = jax.random.fold_in(key, 11)
    perm_key, jitter_key = jax.random.split(sub_key)
    device_keys = jax.random.split(perm_key, DEVICES)
    perms = jax.vmap(lambda one_key: jax.random.permutation(one_key, PTS_DEV))(device_keys).astype(jnp.int32)
    leaf_of = (jnp.arange(POINTS) // LEAF).astype(jnp.float32)
    radius = LEAVES / (8.0 * math.pi)
    angle = 2.0 * math.pi * (leaf_of + 0.5) / LEAVES
    centers = jnp.stack([radius * jnp.cos(angle), radius * jnp.sin(angle), jnp.zeros_like(angle)])
    jitter = jax.random.uniform(jitter_key, (3, POINTS), jnp.float32, -0.5, 0.5)
    sorted_points = centers + jitter
    positions = (jnp.arange(DEVICES, dtype=jnp.int32)[:, None] * PTS_DEV + perms).reshape(-1)
    placed = jnp.zeros((3, POINTS), jnp.float32).at[:, positions].set(sorted_points)
    return (perms.reshape(-1), placed)


def draw_leaf_order(key, part):
    return point_layout(key)[0]


def draw_points(key, part):
    return point_layout(key)[1]


def leaf_lists(key):
    sub_key = jax.random.fold_in(key, 23)
    window = 3 * LD
    scores = jax.random.randint(sub_key, (LEAVES, window), 0, 1 << 20) * window + jnp.arange(window)[None, :]
    own_slot = LD + jnp.arange(LEAVES) % LD
    scores = jnp.where(jnp.arange(window)[None, :] == own_slot[:, None], -1, scores)
    ranked = jnp.argsort(scores, axis=1)
    first_leaf = (jnp.arange(LEAVES) // LD - 1) * LD
    leaf_ids = jnp.mod(first_leaf[:, None] + ranked, LEAVES).astype(jnp.int32)
    return (leaf_ids[:, :NEAR], leaf_ids[:, NEAR:])


def draw_near_list(key, part):
    return leaf_lists(key)[0]


def draw_far_leaf_list(key, part):
    return leaf_lists(key)[1]


def draw_far_chip_list(key, part):
    sub_key = jax.random.fold_in(key, 37)
    score_key, count_key, fullest_key = jax.random.split(sub_key, 3)
    width = 2 * CHIP_SPAN
    scores = jax.random.randint(score_key, (CHIPS, width), 0, 1 << 20) * width + jnp.arange(width)[None, :]
    ranked = jnp.argsort(scores, axis=1)
    distance = jnp.where(ranked < CHIP_SPAN, ranked + 2, -(ranked - CHIP_SPAN + 2))
    targets = jnp.mod(jnp.arange(CHIPS)[:, None] + distance, CHIPS)
    counts = jax.random.randint(count_key, (CHIPS,), 1, width + 1)
    fullest = jax.random.randint(fullest_key, (), 0, CHIPS)
    counts = jnp.where(jnp.arange(CHIPS) == fullest, width, counts)
    live = jnp.arange(width)[None, :] < counts[:, None]
    return jnp.where(live, targets, -1).astype(jnp.int32)


def draw_probes(key, part):
    sub_key = jax.random.fold_in(key, 5)
    base_key, row_key, column_key = jax.random.split(sub_key, 3)
    device_of = (jnp.arange(POINTS) // PTS_DEV).astype(jnp.float32)
    rising = 3.0 ** (device_of / max(DEVICES - 1, 1))
    row_scale = jnp.exp(jax.random.uniform(row_key, (POINTS,), jnp.float32, 0.0, math.log(10.0 / 3.0)))
    column_scale = jnp.exp(jax.random.uniform(column_key, (COLS, 1), jnp.float32, 0.0, math.log(10.0)))
    values = jnp.clip(jax.random.normal(base_key, (COLS, POINTS), jnp.float32), -6.0, 6.0)
    return values * column_scale * (rising * row_scale)[None, :]


def shard_levels(rng, dims, shards, least, top_value):
    loudness = 1.0
    for axis_at, parts in shards:
        draws = jax.random.uniform(jax.random.fold_in(jax.random.fold_in(rng, 6), axis_at), (parts,), jnp.float32, least / len(shards), top_value / len(shards))
        loudness = loudness * jnp.repeat(jnp.exp(draws), dims[axis_at] // parts).reshape((-1,) + (1,) * (len(dims) - 1 - axis_at))
    return loudness


def gaussian(rng, extent, scale, reach, shards=(), kind=jnp.bfloat16):
    drawn = jax.random.normal(rng, extent, jnp.float32) * scale
    if len(shards) > 0:
        drawn = shard_levels(rng, extent, shards, -0.22, 0.18) * drawn
    return jnp.clip(drawn, min=-reach, max=reach).astype(kind)


def setup_inputs(seed: int = 0) -> dict:
    streams_of = jax.random.split(jax.random.key(seed), 11)
    return {
        "probes": draw_probes(jax.random.fold_in(streams_of[10], 71), 0),
        "points": draw_points(jax.random.fold_in(streams_of[10], 71), 0),
        "leaf_order": draw_leaf_order(jax.random.fold_in(streams_of[10], 71), 0),
        "near_list": draw_near_list(jax.random.fold_in(streams_of[10], 71), 0),
        "far_leaf_list": draw_far_leaf_list(jax.random.fold_in(streams_of[10], 71), 0),
        "far_chip_list": draw_far_chip_list(jax.random.fold_in(streams_of[10], 71), 0),
        "leaf_basis": gaussian(streams_of[6], (LEAVES, LEAF, RANK), LEAF ** -0.5, 0.25, ((0, 256),), jnp.float32),
        "transfer": gaussian(streams_of[7], (LEAVES, RANK, RANK), (CHIP_LEAVES * RANK) ** -0.5, 0.1875, ((0, 256),), jnp.float32),
        "far_leaf_blocks": gaussian(streams_of[8], (LEAVES * FARL, RANK, RANK), (FARL * RANK) ** -0.5, 0.25, ((0, 256),), jnp.float32),
        "far_chip_blocks": gaussian(streams_of[9], (CHIPS * FARC, RANK, RANK), (FARC * RANK) ** -0.5, 0.125, ((0, 128),), jnp.float32),
    }


highest = lax.Precision.HIGHEST
inverse_width = 0.5 / (0.15 * 0.15)
epsilon = 1e-06

def kernel_tiles(source_points, target_points):
    spread = source_points[0] - target_points[0]
    distance = spread * spread
    for coord_axis in (1, 2):
        spread = source_points[coord_axis] - target_points[coord_axis]
        distance = distance + spread * spread
    return jnp.exp(-inverse_width * distance)

def apply_matrix(sorted_values, point_tiles, near_list, far_leaf_list, far_chip_list, leaf_basis, transfer, far_leaf_blocks, far_chip_blocks):
    value_tiles = sorted_values.reshape(COLS, LEAVES, LEAF)

    def one_leaf(leaf_id):
        sources = near_list[leaf_id]
        source_points = point_tiles[:, sources]
        target_points = point_tiles[:, leaf_id]
        kernels = kernel_tiles(source_points[..., :, None], target_points[:, None, None, :])
        source_values = value_tiles[:, sources]
        return jnp.einsum('cnp,npq->cq', source_values, kernels, precision=highest)
    near_part = lax.map(one_leaf, jnp.arange(LEAVES, dtype=jnp.int32))
    coefficients = jnp.einsum('clp,lpr->lcr', value_tiles, leaf_basis, precision=highest)
    far_sources = coefficients[far_leaf_list]
    leaf_blocks = far_leaf_blocks.reshape(LEAVES, FARL, RANK, RANK)
    local_far = jnp.einsum('ljcr,ljrs->lcs', far_sources, leaf_blocks, precision=highest)
    upward = jnp.einsum('lcr,lrs->lcs', coefficients, transfer, precision=highest)
    chip_coeffs = lax.optimization_barrier(jnp.sum(upward.reshape(CHIPS, CHIP_LEAVES, COLS, RANK), axis=1))
    valid = far_chip_list >= 0
    safe_ids = jnp.where(valid, far_chip_list, 0)
    chip_sources = chip_coeffs[safe_ids] * valid[:, :, None, None].astype(jnp.float32)
    chip_blocks = far_chip_blocks.reshape(CHIPS, FARC, RANK, RANK)
    chip_far = jnp.einsum('kjcr,kjrs->kcs', chip_sources, chip_blocks, precision=highest)
    per_leaf = jnp.repeat(chip_far, CHIP_LEAVES, axis=0)
    downward = local_far + jnp.einsum('lcs,lrs->lcr', per_leaf, transfer, precision=highest)
    far_part = jnp.einsum('lcr,lpr->lcp', downward, leaf_basis, precision=highest)
    summed_part = near_part + far_part
    return jnp.transpose(summed_part, (1, 0, 2)).reshape(COLS, POINTS)

def reference(probes, points, leaf_order, near_list, far_leaf_list, far_chip_list, leaf_basis, transfer, far_leaf_blocks, far_chip_blocks):
    block_start = jnp.arange(POINTS, dtype=jnp.int32) // PTS_DEV * PTS_DEV
    source_index = (block_start + leaf_order).astype(jnp.int32)
    sorted_probes = probes[:, source_index]
    sorted_points = points[:, source_index]
    point_tiles = sorted_points.reshape(3, LEAVES, LEAF)
    first_pass = apply_matrix(sorted_probes, point_tiles, near_list, far_leaf_list, far_chip_list, leaf_basis, transfer, far_leaf_blocks, far_chip_blocks)
    squares = lax.optimization_barrier(jnp.sum(first_pass * first_pass, axis=1))
    column_scale = lax.rsqrt(squares / POINTS + epsilon)
    second = apply_matrix(first_pass * column_scale[:, None], point_tiles, near_list, far_leaf_list, far_chip_list, leaf_basis, transfer, far_leaf_blocks, far_chip_blocks)
    return jnp.zeros_like(second).at[:, source_index].set(second)
```

```python
import math

import jax
import jax.numpy as jnp
from jax import lax
from jax.experimental import pallas as pl
from jax.experimental.pallas import tpu as pltpu
from jax.sharding import PartitionSpec as P

F32 = jnp.float32
BF16 = jnp.bfloat16
MESH = pl.DeviceIdType.MESH

COLS = 64
LEAF = 512
RANK = 256
CHIPS = 128
LEAVES = 512
DEVICES = 256
POINTS = 262144
NY = 4
NX = 4
NZ = 8
DISTANCES = (2, 3, 4, 5)
EXPONENT = -0.5 / (0.15 * 0.15) * math.log2(math.e)
EPSILON = 1e-6
NN = (((1,), (0,)), ((), ()))
NT = (((1,), (1,)), ((), ()))


def parts_of(x):
    high = x.astype(BF16)
    return high, (x - high.astype(F32)).astype(BF16)


def stacked(x):
    return jnp.concatenate(parts_of(x), axis=0)


def product(both, w_high, w_low, dims=NN):
    rows = both.shape[0] // 2
    main = lax.dot_general(both, w_high, dims, preferred_element_type=F32)
    rest = lax.dot_general(both[:rows], w_low, dims, preferred_element_type=F32)
    return main[:rows] + main[rows:] + rest


def kernel(
    near_ref, far_ref, chip_ref,
    probes_hbm, points_hbm, order_hbm, basis_hbm, transfer_hbm, leafblk_hbm, chipblk_hbm,
    out_ref,
    probes, points, order, basis, transfer, leafblk, chipblk,
    perm, basis_h, basis_l, trans_h, trans_l, leaf_h, leaf_l, chip_h, chip_l,
    kern_h, kern_l, turned, pwin, vwin0, vwin1, cwin0, cwin1,
    gown, grecv, gsum, gchip, hown, hrecv, near, sqown, sqrecv,
    local_sem, send_sem, recv_sem,
):
    vwin = (vwin0, vwin1)
    cwin = (cwin0, cwin1)
    leaf = lax.axis_index("leaf")
    sub = lax.axis_index("sub")
    other = 1 - sub
    dev = 2 * leaf + sub
    sign = 2 * sub - 1
    y = leaf % NY
    x = (leaf // NY) % NX
    z = leaf // (NY * NX)
    nxt = ((dev + 1) % DEVICES) // 2
    prv = ((dev + DEVICES - 1) % DEVICES) // 2

    loads = []
    for n, (src, dst) in enumerate((
        (order_hbm, order), (points_hbm, points), (probes_hbm, probes), (basis_hbm, basis),
        (transfer_hbm, transfer), (chipblk_hbm, chipblk), (leafblk_hbm, leafblk),
    )):
        copy = pltpu.make_async_copy(src, dst, local_sem.at[n])
        copy.start()
        loads.append(copy)
    ld_order, ld_points, ld_probes, ld_basis, ld_transfer, ld_chip, ld_leaf = loads

    def chip_of(dz, dx, dy):
        return (((z + dz) % NZ) * NX + (x + dx) % NX) * NY + (y + dy) % NY

    rounds = (
        [(chip_of(0, 0, dy), (sub + ds) % 2) for dy in range(NY) for ds in range(2) if dy + ds > 0],
        [(chip_of(0, dx, 0), sub) for dx in range(1, NX)],
        [(chip_of(dz, 0, 0), sub) for dz in range(1, NZ)],
    )

    barrier = pltpu.get_barrier_semaphore()
    senders = [(nxt, other), (prv, other)]
    senders += [((leaf - sign * d + CHIPS) % CHIPS, sub) for d in DISTANCES]
    senders += [who for group in rounds for who in group]
    for who in senders:
        pl.semaphore_signal(barrier, inc=1, device_id=who, device_id_type=MESH)

    ld_order.wait()
    row = lax.broadcasted_iota(jnp.int32, (1024, 128), 0)
    for r in range(8):
        perm[:, r * 128:(r + 1) * 128] = (row == order[r:r + 1, :]).astype(F32).astype(BF16)
    ld_points.wait()
    pts = points[...]
    p_1 = pts.astype(BF16).astype(F32)
    p_2 = (pts - p_1).astype(BF16).astype(F32)
    p_3 = (pts - p_1) - p_2
    zero5 = jnp.zeros((5, 1024), F32)
    zero8 = jnp.zeros((8, 1024), F32)
    p_all = jnp.concatenate([p_1, zero5, p_2, zero5, p_3, zero5, zero8], axis=0).astype(BF16)
    p_sorted = lax.dot_general(p_all, perm[...], NN, preferred_element_type=F32)
    p_sorted = (p_sorted[0:8] + p_sorted[8:16]) + p_sorted[16:24]
    for l in range(2):
        pwin[2 + l] = p_sorted[:, l * LEAF:(l + 1) * LEAF]

    pl.semaphore_wait(barrier, len(senders))

    sent = []
    count = [0]

    def send(src, dst, who):
        n = count[0]
        count[0] += 1
        copy = pltpu.make_async_remote_copy(
            src_ref=src, dst_ref=dst, send_sem=send_sem.at[n], recv_sem=recv_sem.at[n],
            device_id=who, device_id_type=MESH,
        )
        copy.start()
        sent.append(copy)
        return copy

    def both_ways(ref):
        return (
            send(ref.at[pl.ds(2, 2)], ref.at[pl.ds(0, 2)], (nxt, other)),
            send(ref.at[pl.ds(2, 2)], ref.at[pl.ds(4, 2)], (prv, other)),
        )

    points_in = both_ways(pwin)

    ld_probes.wait()
    v_sorted = lax.dot_general(stacked(probes[...]), perm[...], NN, preferred_element_type=F32)
    v_sorted = v_sorted[:COLS] + v_sorted[COLS:]
    for l in range(2):
        vwin[0][2 + l] = v_sorted[:, l * LEAF:(l + 1) * LEAF]

    first_leaf = 2 * (dev - 1)

    def place(listed):
        return jnp.clip(lax.rem(listed - first_leaf + 2 * LEAVES, LEAVES), 0, 5)

    def near_place(l, j):
        listed = near_ref[l, j]
        return place(jnp.where(listed == 2 * dev + l, near_ref[l, 3], listed))

    def split_into(src, high, low, at, rows):
        def step(i, _):
            part = pl.ds(pl.multiple_of(i * 64, 64), 64)
            a, b = parts_of(src[at, part, :])
            high[at, part, :] = a
            low[at, part, :] = b
            return 0
        lax.fori_loop(0, rows // 64, step, 0)

    def tile(l, j, source):
        target = pwin[2 + l]
        tx, ty, tz = target[0:1], target[1:2], target[2:3]

        def step(i, _):
            part = pl.ds(pl.multiple_of(i * 32, 32), 32)
            s = turned[source, part, :]
            dx = s[:, 0:1] - tx
            dy = s[:, 1:2] - ty
            dz = s[:, 2:3] - tz
            a, b = parts_of(jnp.exp2((dx * dx + dy * dy + dz * dz) * EXPONENT))
            kern_h[4 * l + j, part, :] = a
            kern_l[4 * l + j, part, :] = b
            return 0
        lax.fori_loop(0, LEAF // 32, step, 0)

    def turn(w):
        whole = jnp.concatenate([pwin[w], jnp.zeros((120, LEAF), F32)], axis=0)
        turned[w] = jnp.transpose(whole)

    def near_term(p, l, j, w):
        return product(stacked(vwin[p][w]), kern_h[4 * l + j], kern_l[4 * l + j])

    def sum_round(r, copies):
        base = (0, 7, 10)[r]
        for i, copy in enumerate(copies):
            copy.wait_recv()
        total = sqown[r]
        for i in range(len(copies)):
            total = total + sqrecv[base + i]
        return total

    def start_round(r, total):
        base = (0, 7, 10)[r]
        sqown[r] = total
        return [send(sqown.at[r], sqrecv.at[base + i], who) for i, who in enumerate(rounds[r])]

    squares = None
    for p in range(2):
        if p == 0:
            ld_basis.wait()
            for l in range(2):
                split_into(basis, basis_h, basis_l, l, LEAF)
        up = []
        for l in range(2):
            c = product(stacked(vwin[p][2 + l]), basis_h[l], basis_l[l])
            cwin[p][2 + l] = c
            up.append(c)
        if p == 0:
            ld_transfer.wait()
            for l in range(2):
                split_into(transfer, trans_h, trans_l, l, RANK)
        gown[p] = sum(product(stacked(up[l]), trans_h[l], trans_l[l]) for l in range(2))
        g_in = send(gown.at[p], grecv.at[p], (leaf, other))
        values_in = None
        if p == 0:
            values_in = both_ways(vwin[p])
            for l in range(2):
                turn(2 + l)
        if p == 0:
            for l in range(2):
                tile(l, 3, 2 + l)
        g_in.wait_recv()
        gsum[p] = gown[p] + grecv[p]
        chips_in = [
            send(gsum.at[p], gchip.at[p, i], ((leaf + sign * d + CHIPS) % CHIPS, sub))
            for i, d in enumerate(DISTANCES)
        ]
        if values_in is None:
            values_in = both_ways(vwin[p])
        coeff_in = both_ways(cwin[p])
        if p == 1:
            v = jnp.concatenate([vwin[p][2], vwin[p][3]], axis=1)
            v = v * v
            total = lax.dot_general(
                jnp.ones((8, 1024), F32), jnp.concatenate([v, v], axis=0), NT,
                precision=lax.Precision.HIGHEST, preferred_element_type=F32,
            )
            squares = start_round(0, total)
        for l in range(2):
            near[l] = near_term(p, l, 3, 2 + l)
        if p == 0:
            ld_chip.wait()
            for i, d in enumerate(DISTANCES):
                want = jnp.where(sub == 0, d, CHIPS - d)
                slot = jnp.int32(0)
                found = jnp.int32(0)
                for j in range(8):
                    listed = chip_ref[0, j]
                    hit = jnp.where(
                        (listed >= 0) & (lax.rem(listed - leaf + CHIPS, CHIPS) == want), 1, 0
                    )
                    slot = slot + j * hit
                    found = found + hit
                slot = jnp.clip(slot, 0, 7)
                weight = found.astype(F32)

                def step(k, _, i=i, slot=slot, weight=weight):
                    part = pl.ds(pl.multiple_of(k * 64, 64), 64)
                    a, b = parts_of(chipblk[slot, part, :] * weight)
                    chip_h[i, part, :] = a
                    chip_l[i, part, :] = b
                    return 0
                lax.fori_loop(0, RANK // 64, step, 0)
            ld_leaf.wait()
            for n in range(4):
                split_into(leafblk, leaf_h, leaf_l, n, RANK)
            for copy in points_in:
                copy.wait_recv()
            for w in (0, 1, 4, 5):
                turn(w)
            for l in range(2):
                for j in range(3):
                    tile(l, j, near_place(l, j))
        for copy in chips_in:
            copy.wait_recv()
        hown[p] = sum(product(stacked(gchip[p, i]), chip_h[i], chip_l[i]) for i in range(4))
        h_in = send(hown.at[p], hrecv.at[p], (leaf, other))
        if p == 1:
            squares = start_round(1, sum_round(0, squares))
        for copy in values_in:
            copy.wait_recv()
        for l in range(2):
            near[l] = near[l] + sum(near_term(p, l, j, near_place(l, j)) for j in range(3))
        for copy in coeff_in:
            copy.wait_recv()
        local = [
            sum(
                product(stacked(cwin[p][place(far_ref[l, j])]), leaf_h[2 * l + j], leaf_l[2 * l + j])
                for j in range(2)
            )
            for l in range(2)
        ]
        if p == 1:
            squares = start_round(2, sum_round(1, squares))
        h_in.wait_recv()
        h = stacked(hown[p] + hrecv[p])
        done = []
        for l in range(2):
            e = local[l] + product(h, trans_h[l], trans_l[l], NT)
            done.append(near[l] + product(stacked(e), basis_h[l], basis_l[l], NT))
        if p == 0:
            for l in range(2):
                vwin[1][2 + l] = done[l]
        else:
            second = stacked(jnp.concatenate(done, axis=1))
            placed = lax.dot_general(second, perm[...], NT, preferred_element_type=F32)
            total = sum_round(2, squares)
            scale = lax.rsqrt(total * (1.0 / POINTS) + EPSILON)
            wide = jnp.broadcast_to(scale[0:1, :], (COLS, 128))
            diagonal = lax.broadcasted_iota(jnp.int32, (COLS, 128), 0) == lax.broadcasted_iota(
                jnp.int32, (COLS, 128), 1
            )
            column = jnp.sum(jnp.where(diagonal, wide, 0.0), axis=1, keepdims=True)
            out_ref[...] = (placed[:COLS] + placed[COLS:]) * column
    for copy in sent:
        copy.wait_send()


def on_device(
    probes, points, leaf_order, near_list, far_leaf_list, far_chip_list,
    leaf_basis, transfer, far_leaf_blocks, far_chip_blocks,
):
    smem = pl.BlockSpec(memory_space=pltpu.SMEM)
    anywhere = pl.BlockSpec(memory_space=pl.ANY)
    vmem = pltpu.VMEM
    dma = pltpu.SemaphoreType.DMA
    return pl.pallas_call(
        kernel,
        out_shape=jax.ShapeDtypeStruct((COLS, 1024), F32),
        in_specs=[smem] * 3 + [anywhere] * 7,
        out_specs=pl.BlockSpec(memory_space=pltpu.VMEM),
        scratch_shapes=[
            vmem((COLS, 1024), F32),
            vmem((3, 1024), F32),
            vmem((8, 128), jnp.int32),
            vmem((2, LEAF, RANK), F32),
            vmem((2, RANK, RANK), F32),
            vmem((4, RANK, RANK), F32),
            vmem((8, RANK, RANK), F32),
            vmem((1024, 1024), BF16),
            vmem((2, LEAF, RANK), BF16),
            vmem((2, LEAF, RANK), BF16),
            vmem((2, RANK, RANK), BF16),
            vmem((2, RANK, RANK), BF16),
            vmem((4, RANK, RANK), BF16),
            vmem((4, RANK, RANK), BF16),
            vmem((4, RANK, RANK), BF16),
            vmem((4, RANK, RANK), BF16),
            vmem((8, LEAF, LEAF), BF16),
            vmem((8, LEAF, LEAF), BF16),
            vmem((6, LEAF, 128), F32),
            vmem((6, 8, LEAF), F32),
            vmem((6, COLS, LEAF), F32),
            vmem((6, COLS, LEAF), F32),
            vmem((6, COLS, RANK), F32),
            vmem((6, COLS, RANK), F32),
            vmem((2, COLS, RANK), F32),
            vmem((2, COLS, RANK), F32),
            vmem((2, COLS, RANK), F32),
            vmem((2, 4, COLS, RANK), F32),
            vmem((2, COLS, RANK), F32),
            vmem((2, COLS, RANK), F32),
            vmem((2, COLS, LEAF), F32),
            vmem((3, 8, 128), F32),
            vmem((17, 8, 128), F32),
            dma((7,)),
            dma((39,)),
            dma((39,)),
        ],
        compiler_params=pltpu.CompilerParams(
            collective_id=0, has_side_effects=True, vmem_limit_bytes=56 * 1024 * 1024
        ),
    )(
        near_list, far_leaf_list, far_chip_list, probes, points, leaf_order.reshape(8, 128),
        leaf_basis, transfer, far_leaf_blocks, far_chip_blocks,
    )


def solution(mesh):
    both = ("leaf", "sub")
    return jax.shard_map(
        on_device,
        mesh=mesh,
        in_specs=(
            P(None, both), P(None, both), P(both), P(both, None), P(both, None), P("leaf", None),
            P(both, None, None), P(both, None, None), P(both, None, None), P("leaf", None, None),
        ),
        out_specs=P(None, both),
        check_vma=False,
    )
```

```python
import math

import jax
import jax.numpy as jnp
from jax import lax
from jax.experimental import pallas as pl
from jax.experimental.pallas import tpu as pltpu
from jax.sharding import PartitionSpec as P

F32 = jnp.float32
BF16 = jnp.bfloat16
MESH = pl.DeviceIdType.MESH

COLS = 64
LEAF = 512
RANK = 256
CHIPS = 128
LEAVES = 512
DEVICES = 256
POINTS = 262144
NY = 4
NX = 4
NZ = 8
DISTANCES = (2, 3, 4, 5)
EXPONENT = -0.5 / (0.15 * 0.15) * math.log2(math.e)
EPSILON = 1e-6
NN = (((1,), (0,)), ((), ()))
NT = (((1,), (1,)), ((), ()))


def parts_of(x):
    high = x.astype(BF16)
    return high, (x - high.astype(F32)).astype(BF16)


def stacked(x):
    return jnp.concatenate(parts_of(x), axis=0)


def product(both, w_high, w_low, dims=NN):
    rows = both.shape[0] // 2
    main = lax.dot_general(both, w_high, dims, preferred_element_type=F32)
    rest = lax.dot_general(both[:rows], w_low, dims, preferred_element_type=F32)
    return main[:rows] + main[rows:] + rest


def kernel(
    near_ref, far_ref, chip_ref,
    probes_hbm, points_hbm, order_hbm, basis_hbm, transfer_hbm, leafblk_hbm, chipblk_hbm,
    out_ref,
    probes, points, order, basis, transfer, leafblk, chipblk,
    perm, basis_h, basis_l, trans_h, trans_l, leaf_h, leaf_l, chip_h, chip_l,
    kern_h, kern_l, turned, pwin, vwin0, vwin1, cwin0, cwin1,
    gown, grecv, gsum, gchip, hown, hrecv, near, sqown, sqrecv,
    local_sem, send_sem, recv_sem,
):
    vwin = (vwin0, vwin1)
    cwin = (cwin0, cwin1)
    leaf = lax.axis_index("leaf")
    sub = lax.axis_index("sub")
    other = 1 - sub
    dev = 2 * leaf + sub
    sign = 2 * sub - 1
    y = leaf % NY
    x = (leaf // NY) % NX
    z = leaf // (NY * NX)
    nxt = ((dev + 1) % DEVICES) // 2
    prv = ((dev + DEVICES - 1) % DEVICES) // 2

    loads = []
    for n, (src, dst) in enumerate((
        (order_hbm, order), (points_hbm, points), (probes_hbm, probes), (basis_hbm, basis),
        (transfer_hbm, transfer), (chipblk_hbm, chipblk), (leafblk_hbm, leafblk),
    )):
        copy = pltpu.make_async_copy(src, dst, local_sem.at[n])
        copy.start()
        loads.append(copy)
    ld_order, ld_points, ld_probes, ld_basis, ld_transfer, ld_chip, ld_leaf = loads

    def chip_of(dz, dx, dy):
        return (((z + dz) % NZ) * NX + (x + dx) % NX) * NY + (y + dy) % NY

    rounds = (
        [(chip_of(0, dx, dy), sub) for dx in range(NX) for dy in range(NY) if dx + dy > 0],
        [(chip_of(dz, 0, 0), (sub + ds) % 2) for dz in range(NZ) for ds in range(2) if dz + ds > 0],
    )

    barrier = pltpu.get_barrier_semaphore()
    senders = [(nxt, other), (prv, other)]
    senders += [((leaf - sign * d + CHIPS) % CHIPS, sub) for d in DISTANCES]
    senders += [who for group in rounds for who in group]
    for who in senders:
        pl.semaphore_signal(barrier, inc=1, device_id=who, device_id_type=MESH)

    ld_order.wait()
    row = lax.broadcasted_iota(jnp.int32, (1024, 128), 0)
    for r in range(8):
        perm[:, r * 128:(r + 1) * 128] = (row == order[r:r + 1, :]).astype(F32).astype(BF16)
    ld_points.wait()
    pts = points[...]
    p_1 = pts.astype(BF16).astype(F32)
    p_2 = (pts - p_1).astype(BF16).astype(F32)
    p_3 = (pts - p_1) - p_2
    zero5 = jnp.zeros((5, 1024), F32)
    zero8 = jnp.zeros((8, 1024), F32)
    p_all = jnp.concatenate([p_1, zero5, p_2, zero5, p_3, zero5, zero8], axis=0).astype(BF16)
    p_sorted = lax.dot_general(p_all, perm[...], NN, preferred_element_type=F32)
    p_sorted = (p_sorted[0:8] + p_sorted[8:16]) + p_sorted[16:24]
    for l in range(2):
        pwin[2 + l] = p_sorted[:, l * LEAF:(l + 1) * LEAF]

    pl.semaphore_wait(barrier, len(senders))

    sent = []
    count = [0]

    def send(src, dst, who):
        n = count[0]
        count[0] += 1
        copy = pltpu.make_async_remote_copy(
            src_ref=src, dst_ref=dst, send_sem=send_sem.at[n], recv_sem=recv_sem.at[n],
            device_id=who, device_id_type=MESH,
        )
        copy.start()
        sent.append(copy)
        return copy

    def both_ways(ref, at=2, n=2):
        return [
            send(ref.at[pl.ds(at, n)], ref.at[pl.ds(at - 2, n)], (nxt, other)),
            send(ref.at[pl.ds(at, n)], ref.at[pl.ds(at + 2, n)], (prv, other)),
        ]

    points_in = both_ways(pwin)

    ld_probes.wait()
    v_sorted = lax.dot_general(stacked(probes[...]), perm[...], NN, preferred_element_type=F32)
    v_sorted = v_sorted[:COLS] + v_sorted[COLS:]
    for l in range(2):
        vwin[0][2 + l] = v_sorted[:, l * LEAF:(l + 1) * LEAF]

    first_leaf = 2 * (dev - 1)

    def place(listed):
        return jnp.clip(lax.rem(listed - first_leaf + 2 * LEAVES, LEAVES), 0, 5)

    def near_place(l, j):
        listed = near_ref[l, j]
        return place(jnp.where(listed == 2 * dev + l, near_ref[l, 3], listed))

    def split_into(src, high, low, at, rows):
        def step(i, _):
            part = pl.ds(pl.multiple_of(i * 64, 64), 64)
            a, b = parts_of(src[at, part, :])
            high[at, part, :] = a
            low[at, part, :] = b
            return 0
        lax.fori_loop(0, rows // 64, step, 0)

    def tile(l, j, source):
        target = pwin[2 + l]
        tx, ty, tz = target[0:1], target[1:2], target[2:3]

        def step(i, _):
            part = pl.ds(pl.multiple_of(i * 64, 64), 64)
            s = turned[source, part, :]
            dx = s[:, 0:1] - tx
            dy = s[:, 1:2] - ty
            dz = s[:, 2:3] - tz
            a, b = parts_of(jnp.exp2((dx * dx + dy * dy + dz * dz) * EXPONENT))
            kern_h[4 * l + j, part, :] = a
            kern_l[4 * l + j, part, :] = b
            return 0
        lax.fori_loop(0, LEAF // 64, step, 0, unroll=4)

    def turn(w):
        whole = jnp.concatenate([pwin[w], jnp.zeros((120, LEAF), F32)], axis=0)
        turned[w] = jnp.transpose(whole)

    def near_term(p, l, j, w):
        return product(stacked(vwin[p][w]), kern_h[4 * l + j], kern_l[4 * l + j])

    def sum_round(r, copies):
        base = 15 * r
        for i, copy in enumerate(copies):
            copy.wait_recv()
        total = sqown[r]
        for i in range(len(copies)):
            total = total + sqrecv[base + i]
        return total

    def start_round(r, total):
        base = 15 * r
        sqown[r] = total
        return [send(sqown.at[r], sqrecv.at[base + i], who) for i, who in enumerate(rounds[r])]

    squares = None
    for p in range(2):
        if p == 0:
            ld_basis.wait()
            for l in range(2):
                split_into(basis, basis_h, basis_l, l, LEAF)
        up = []
        for l in range(2):
            c = product(stacked(vwin[p][2 + l]), basis_h[l], basis_l[l])
            cwin[p][2 + l] = c
            up.append(c)
        if p == 0:
            ld_transfer.wait()
            for l in range(2):
                split_into(transfer, trans_h, trans_l, l, RANK)
        gown[p] = sum(product(stacked(up[l]), trans_h[l], trans_l[l]) for l in range(2))
        g_in = send(gown.at[p], grecv.at[p], (leaf, other))
        if p == 0:
            for l in range(2):
                turn(2 + l)
            for l in range(2):
                tile(l, 3, 2 + l)
        else:
            values_in = ahead + both_ways(vwin[1], 3, 1)
            total = jnp.zeros((COLS, 128), F32)
            for l in range(2):
                v = vwin[1][2 + l]
                v = v * v
                for k in range(4):
                    total = total + v[:, k * 128:(k + 1) * 128]
            total = lax.dot_general(
                jnp.ones((8, 128), F32), jnp.concatenate([total, total], axis=0), NT,
                precision=lax.Precision.HIGHEST, preferred_element_type=F32,
            )
            squares = start_round(0, total)
        g_in.wait_recv()
        gsum[p] = gown[p] + grecv[p]
        chips_in = [
            send(gsum.at[p], gchip.at[p, i], ((leaf + sign * d + CHIPS) % CHIPS, sub))
            for i, d in enumerate(DISTANCES)
        ]
        if p == 0:
            values_in = both_ways(vwin[0])
        coeff_in = both_ways(cwin[p])
        for l in range(2):
            near[l] = near_term(p, l, 3, 2 + l)
        if p == 1:
            squares = start_round(1, sum_round(0, squares))
        if p == 0:
            ld_chip.wait()
            for i, d in enumerate(DISTANCES):
                want = jnp.where(sub == 0, d, CHIPS - d)
                slot = jnp.int32(0)
                found = jnp.int32(0)
                for j in range(8):
                    listed = chip_ref[0, j]
                    hit = jnp.where(
                        (listed >= 0) & (lax.rem(listed - leaf + CHIPS, CHIPS) == want), 1, 0
                    )
                    slot = slot + j * hit
                    found = found + hit
                slot = jnp.clip(slot, 0, 7)
                weight = found.astype(F32)

                def step(k, _, i=i, slot=slot, weight=weight):
                    part = pl.ds(pl.multiple_of(k * 64, 64), 64)
                    a, b = parts_of(chipblk[slot, part, :] * weight)
                    chip_h[i, part, :] = a
                    chip_l[i, part, :] = b
                    return 0
                lax.fori_loop(0, RANK // 64, step, 0)
            ld_leaf.wait()
            for n in range(4):
                split_into(leafblk, leaf_h, leaf_l, n, RANK)
            for copy in points_in:
                copy.wait_recv()
            for w in (0, 1, 4, 5):
                turn(w)
            for l in range(2):
                for j in range(3):
                    tile(l, j, near_place(l, j))
        for copy in chips_in:
            copy.wait_recv()
        hown[p] = sum(product(stacked(gchip[p, i]), chip_h[i], chip_l[i]) for i in range(4))
        h_in = send(hown.at[p], hrecv.at[p], (leaf, other))
        for copy in values_in:
            copy.wait_recv()
        for l in range(2):
            near[l] = near[l] + sum(near_term(p, l, j, near_place(l, j)) for j in range(3))
        for copy in coeff_in:
            copy.wait_recv()
        local = [
            sum(
                product(stacked(cwin[p][place(far_ref[l, j])]), leaf_h[2 * l + j], leaf_l[2 * l + j])
                for j in range(2)
            )
            for l in range(2)
        ]
        h_in.wait_recv()
        h = stacked(hown[p] + hrecv[p])
        done = []
        for l in range(2):
            e = local[l] + product(h, trans_h[l], trans_l[l], NT)
            done.append(near[l] + product(stacked(e), basis_h[l], basis_l[l], NT))
            if p == 0:
                vwin[1][2 + l] = done[l]
                if l == 0:
                    ahead = both_ways(vwin[1], 2, 1)
        if p == 1:
            second = stacked(jnp.concatenate(done, axis=1))
            placed = lax.dot_general(second, perm[...], NT, preferred_element_type=F32)
            total = sum_round(1, squares)
            scale = lax.rsqrt(total * (1.0 / POINTS) + EPSILON)
            wide = jnp.broadcast_to(scale[0:1, :], (COLS, 128))
            diagonal = lax.broadcasted_iota(jnp.int32, (COLS, 128), 0) == lax.broadcasted_iota(
                jnp.int32, (COLS, 128), 1
            )
            column = jnp.sum(jnp.where(diagonal, wide, 0.0), axis=1, keepdims=True)
            out_ref[...] = (placed[:COLS] + placed[COLS:]) * column
    for copy in sent:
        copy.wait_send()


def on_device(
    probes, points, leaf_order, near_list, far_leaf_list, far_chip_list,
    leaf_basis, transfer, far_leaf_blocks, far_chip_blocks,
):
    smem = pl.BlockSpec(memory_space=pltpu.SMEM)
    anywhere = pl.BlockSpec(memory_space=pl.ANY)
    vmem = pltpu.VMEM
    dma = pltpu.SemaphoreType.DMA
    return pl.pallas_call(
        kernel,
        out_shape=jax.ShapeDtypeStruct((COLS, 1024), F32),
        in_specs=[smem] * 3 + [anywhere] * 7,
        out_specs=pl.BlockSpec(memory_space=pltpu.VMEM),
        scratch_shapes=[
            vmem((COLS, 1024), F32),
            vmem((3, 1024), F32),
            vmem((8, 128), jnp.int32),
            vmem((2, LEAF, RANK), F32),
            vmem((2, RANK, RANK), F32),
            vmem((4, RANK, RANK), F32),
            vmem((8, RANK, RANK), F32),
            vmem((1024, 1024), BF16),
            vmem((2, LEAF, RANK), BF16),
            vmem((2, LEAF, RANK), BF16),
            vmem((2, RANK, RANK), BF16),
            vmem((2, RANK, RANK), BF16),
            vmem((4, RANK, RANK), BF16),
            vmem((4, RANK, RANK), BF16),
            vmem((4, RANK, RANK), BF16),
            vmem((4, RANK, RANK), BF16),
            vmem((8, LEAF, LEAF), BF16),
            vmem((8, LEAF, LEAF), BF16),
            vmem((6, LEAF, 128), F32),
            vmem((6, 8, LEAF), F32),
            vmem((6, COLS, LEAF), F32),
            vmem((6, COLS, LEAF), F32),
            vmem((6, COLS, RANK), F32),
            vmem((6, COLS, RANK), F32),
            vmem((2, COLS, RANK), F32),
            vmem((2, COLS, RANK), F32),
            vmem((2, COLS, RANK), F32),
            vmem((2, 4, COLS, RANK), F32),
            vmem((2, COLS, RANK), F32),
            vmem((2, COLS, RANK), F32),
            vmem((2, COLS, LEAF), F32),
            vmem((2, 8, 128), F32),
            vmem((30, 8, 128), F32),
            dma((7,)),
            dma((54,)),
            dma((54,)),
        ],
        compiler_params=pltpu.CompilerParams(
            collective_id=0, has_side_effects=True, vmem_limit_bytes=56 * 1024 * 1024
        ),
    )(
        near_list, far_leaf_list, far_chip_list, probes, points, leaf_order.reshape(8, 128),
        leaf_basis, transfer, far_leaf_blocks, far_chip_blocks,
    )


def solution(mesh):
    both = ("leaf", "sub")
    return jax.shard_map(
        on_device,
        mesh=mesh,
        in_specs=(
            P(None, both), P(None, both), P(both), P(both, None), P(both, None), P("leaf", None),
            P(both, None, None), P(both, None, None), P(both, None, None), P("leaf", None, None),
        ),
        out_specs=P(None, both),
        check_vma=False,
    )
```

```python
import math

import jax
import jax.numpy as jnp
from jax import lax
from jax.experimental import pallas as pl
from jax.experimental.pallas import tpu as pltpu
from jax.sharding import PartitionSpec as P

F32 = jnp.float32
BF16 = jnp.bfloat16
MESH = pl.DeviceIdType.MESH

COLS = 64
LEAF = 512
RANK = 256
CHIPS = 128
LEAVES = 512
DEVICES = 256
POINTS = 262144
NY = 4
NX = 4
NZ = 8
DISTANCES = (5, 2, 3, 4)
EXPONENT = -0.5 / (0.15 * 0.15) * math.log2(math.e)
EPSILON = 1e-6
NN = (((1,), (0,)), ((), ()))
NT = (((1,), (1,)), ((), ()))


def parts_of(x):
    high = x.astype(BF16)
    return high, (x - high.astype(F32)).astype(BF16)


def stacked(x):
    return jnp.concatenate(parts_of(x), axis=0)


def product(both, w_high, w_low, dims=NN):
    rows = both.shape[0] // 2
    main = lax.dot_general(both, w_high, dims, preferred_element_type=F32)
    rest = lax.dot_general(both[:rows], w_low, dims, preferred_element_type=F32)
    return main[:rows] + main[rows:] + rest


def kernel(
    near_ref, far_ref, chip_ref,
    probes_hbm, points_hbm, order_hbm, basis_hbm, transfer_hbm, leafblk_hbm, chipblk_hbm,
    out_ref,
    probes, points, order, basis, transfer, leafblk, chipblk,
    perm, basis_h, basis_l, trans_h, trans_l, leaf_h, leaf_l, chip_h, chip_l,
    kern_h, kern_l, turned, pwin, vwin0, vwin1, cwin0, cwin1,
    gown, grecv, gsum, gchip, hown, hrecv, near, sqown, sqrecv,
    local_sem, send_sem, recv_sem,
):
    vwin = (vwin0, vwin1)
    cwin = (cwin0, cwin1)
    leaf = lax.axis_index("leaf")
    sub = lax.axis_index("sub")
    other = 1 - sub
    dev = 2 * leaf + sub
    sign = 2 * sub - 1
    y = leaf % NY
    x = (leaf // NY) % NX
    z = leaf // (NY * NX)
    across = (leaf + sign + CHIPS) % CHIPS

    loads = []
    for n, (src, dst) in enumerate((
        (order_hbm, order), (points_hbm, points), (probes_hbm, probes), (basis_hbm, basis),
        (transfer_hbm, transfer), (chipblk_hbm, chipblk), (leafblk_hbm, leafblk),
    )):
        copy = pltpu.make_async_copy(src, dst, local_sem.at[n])
        copy.start()
        loads.append(copy)
    ld_order, ld_points, ld_probes, ld_basis, ld_transfer, ld_chip, ld_leaf = loads

    def chip_of(dz, dx, dy):
        return (((z + dz) % NZ) * NX + (x + dx) % NX) * NY + (y + dy) % NY

    rounds = (
        [(chip_of(0, dx, dy), sub) for dx in range(NX) for dy in range(NY) if dx + dy > 0],
        [(chip_of(dz, 0, 0), (sub + ds) % 2) for dz in range(NZ) for ds in range(2) if dz + ds > 0],
    )

    barrier = pltpu.get_barrier_semaphore()
    senders = [(across, other), (leaf, other)]
    senders += [((leaf - sign * d + CHIPS) % CHIPS, sub) for d in DISTANCES]
    senders += [who for group in rounds for who in group]
    for who in senders:
        pl.semaphore_signal(barrier, inc=1, device_id=who, device_id_type=MESH)

    ld_order.wait()
    row = lax.broadcasted_iota(jnp.int32, (1024, 128), 0)
    for r in range(8):
        perm[:, r * 128:(r + 1) * 128] = (row == order[r:r + 1, :]).astype(F32).astype(BF16)
    ld_points.wait()
    pts = points[...]
    p_1 = pts.astype(BF16).astype(F32)
    p_2 = (pts - p_1).astype(BF16).astype(F32)
    p_3 = (pts - p_1) - p_2
    zero5 = jnp.zeros((5, 1024), F32)
    zero8 = jnp.zeros((8, 1024), F32)
    p_all = jnp.concatenate([p_1, zero5, p_2, zero5, p_3, zero5, zero8], axis=0).astype(BF16)
    p_sorted = lax.dot_general(p_all, perm[...], NN, preferred_element_type=F32)
    p_sorted = (p_sorted[0:8] + p_sorted[8:16]) + p_sorted[16:24]
    for l in range(2):
        pwin[2 + l] = p_sorted[:, l * LEAF:(l + 1) * LEAF]

    pl.semaphore_wait(barrier, len(senders))

    sent = []
    count = [0]

    def send(src, dst, who):
        n = count[0]
        count[0] += 1
        copy = pltpu.make_async_remote_copy(
            src_ref=src, dst_ref=dst, send_sem=send_sem.at[n], recv_sem=recv_sem.at[n],
            device_id=who, device_id_type=MESH,
        )
        copy.start()
        sent.append(copy)
        return copy

    def both_ways(ref, at=2, n=2):
        return [
            send(ref.at[pl.ds(at, n)], ref.at[pl.ds(at + 2 - 4 * sub, n)], (across, other)),
            send(ref.at[pl.ds(at, n)], ref.at[pl.ds(at - 2 + 4 * sub, n)], (leaf, other)),
        ]

    points_in = both_ways(pwin)

    ld_probes.wait()
    v_sorted = lax.dot_general(stacked(probes[...]), perm[...], NN, preferred_element_type=F32)
    v_sorted = v_sorted[:COLS] + v_sorted[COLS:]
    for l in range(2):
        vwin[0][2 + l] = v_sorted[:, l * LEAF:(l + 1) * LEAF]
    values_in = both_ways(vwin[0])

    first_leaf = 2 * (dev - 1)

    def place(listed):
        return jnp.clip(lax.rem(listed - first_leaf + 2 * LEAVES, LEAVES), 0, 5)

    def near_place(l, j):
        listed = near_ref[l, j]
        return place(jnp.where(listed == 2 * dev + l, near_ref[l, 3], listed))

    def split_into(src, high, low, at, rows):
        def step(i, _):
            part = pl.ds(pl.multiple_of(i * 64, 64), 64)
            a, b = parts_of(src[at, part, :])
            high[at, part, :] = a
            low[at, part, :] = b
            return 0
        lax.fori_loop(0, rows // 64, step, 0)

    def tile(l, j, source):
        target = pwin[2 + l]
        tx, ty, tz = target[0:1], target[1:2], target[2:3]

        def step(i, _):
            part = pl.ds(pl.multiple_of(i * 64, 64), 64)
            s = turned[source, part, :]
            dx = s[:, 0:1] - tx
            dy = s[:, 1:2] - ty
            dz = s[:, 2:3] - tz
            a, b = parts_of(jnp.exp2((dx * dx + dy * dy + dz * dz) * EXPONENT))
            kern_h[4 * l + j, part, :] = a
            kern_l[4 * l + j, part, :] = b
            return 0
        lax.fori_loop(0, LEAF // 64, step, 0, unroll=4)

    def turn(w):
        whole = jnp.concatenate([pwin[w], jnp.zeros((120, LEAF), F32)], axis=0)
        turned[w] = jnp.transpose(whole)

    def near_term(p, l, j, w):
        return product(stacked(vwin[p][w]), kern_h[4 * l + j], kern_l[4 * l + j])

    def sum_round(r, copies):
        base = 15 * r
        for i, copy in enumerate(copies):
            copy.wait_recv()
        total = sqown[r]
        for i in range(len(copies)):
            total = total + sqrecv[base + i]
        return total

    def start_round(r, total):
        base = 15 * r
        sqown[r] = total
        return [send(sqown.at[r], sqrecv.at[base + i], who) for i, who in enumerate(rounds[r])]

    squares = None
    for p in range(2):
        if p == 0:
            ld_basis.wait()
            for l in range(2):
                split_into(basis, basis_h, basis_l, l, LEAF)
        up = []
        for l in range(2):
            c = product(stacked(vwin[p][2 + l]), basis_h[l], basis_l[l])
            cwin[p][2 + l] = c
            up.append(c)
        if p == 0:
            ld_transfer.wait()
            for l in range(2):
                split_into(transfer, trans_h, trans_l, l, RANK)
        gown[p] = sum(product(stacked(up[l]), trans_h[l], trans_l[l]) for l in range(2))
        g_in = send(gown.at[p], grecv.at[p], (leaf, other))
        if p == 0:
            for l in range(2):
                turn(2 + l)
            ld_chip.wait()
            for i, d in enumerate(DISTANCES):
                want = jnp.where(sub == 0, d, CHIPS - d)
                slot = jnp.int32(0)
                found = jnp.int32(0)
                for j in range(8):
                    listed = chip_ref[0, j]
                    hit = jnp.where(
                        (listed >= 0) & (lax.rem(listed - leaf + CHIPS, CHIPS) == want), 1, 0
                    )
                    slot = slot + j * hit
                    found = found + hit
                slot = jnp.clip(slot, 0, 7)
                weight = found.astype(F32)

                def step(k, _, i=i, slot=slot, weight=weight):
                    part = pl.ds(pl.multiple_of(k * 64, 64), 64)
                    a, b = parts_of(chipblk[slot, part, :] * weight)
                    chip_h[i, part, :] = a
                    chip_l[i, part, :] = b
                    return 0
                lax.fori_loop(0, RANK // 64, step, 0)
            ld_leaf.wait()
            for n in range(4):
                split_into(leafblk, leaf_h, leaf_l, n, RANK)
        else:
            values_in = ahead
            total = jnp.zeros((COLS, 128), F32)
            for l in range(2):
                v = vwin[1][2 + l]
                v = v * v
                for k in range(4):
                    total = total + v[:, k * 128:(k + 1) * 128]
            total = lax.dot_general(
                jnp.ones((8, 128), F32), jnp.concatenate([total, total], axis=0), NT,
                precision=lax.Precision.HIGHEST, preferred_element_type=F32,
            )
            squares = start_round(0, total)
        g_in.wait_recv()
        gsum[p] = gown[p] + grecv[p]
        chips_in = [
            send(gsum.at[p], gchip.at[p, i], ((leaf + sign * d + CHIPS) % CHIPS, sub))
            for i, d in enumerate(DISTANCES)
        ]
        coeff_in = both_ways(cwin[p])
        if p == 0:
            for l in range(2):
                tile(l, 3, 2 + l)
        for l in range(2):
            near[l] = near_term(p, l, 3, 2 + l)
        if p == 1:
            squares = start_round(1, sum_round(0, squares))
        if p == 0:
            for copy in points_in:
                copy.wait_recv()
            for w in (0, 1, 4, 5):
                turn(w)
            for l in range(2):
                for j in range(3):
                    tile(l, j, near_place(l, j))
        for copy in chips_in:
            copy.wait_recv()
        hown[p] = sum(product(stacked(gchip[p, i]), chip_h[i], chip_l[i]) for i in range(4))
        h_in = send(hown.at[p], hrecv.at[p], (leaf, other))
        for copy in values_in:
            copy.wait_recv()
        for l in range(2):
            near[l] = near[l] + sum(near_term(p, l, j, near_place(l, j)) for j in range(3))
        for copy in coeff_in:
            copy.wait_recv()
        local = [
            sum(
                product(stacked(cwin[p][place(far_ref[l, j])]), leaf_h[2 * l + j], leaf_l[2 * l + j])
                for j in range(2)
            )
            for l in range(2)
        ]
        h_in.wait_recv()
        h = stacked(hown[p] + hrecv[p])
        done = []
        for l in range(2):
            e = local[l] + product(h, trans_h[l], trans_l[l], NT)
            done.append(near[l] + product(stacked(e), basis_h[l], basis_l[l], NT))
            if p == 0:
                vwin[1][2 + l] = done[l]
                ahead = (ahead if l else []) + both_ways(vwin[1], 2 + l, 1)
        if p == 1:
            second = stacked(jnp.concatenate(done, axis=1))
            placed = lax.dot_general(second, perm[...], NT, preferred_element_type=F32)
            total = sum_round(1, squares)
            scale = lax.rsqrt(total * (1.0 / POINTS) + EPSILON)
            wide = jnp.broadcast_to(scale[0:1, :], (COLS, 128))
            diagonal = lax.broadcasted_iota(jnp.int32, (COLS, 128), 0) == lax.broadcasted_iota(
                jnp.int32, (COLS, 128), 1
            )
            column = jnp.sum(jnp.where(diagonal, wide, 0.0), axis=1, keepdims=True)
            out_ref[...] = (placed[:COLS] + placed[COLS:]) * column
    for copy in sent:
        copy.wait_send()


def on_device(
    probes, points, leaf_order, near_list, far_leaf_list, far_chip_list,
    leaf_basis, transfer, far_leaf_blocks, far_chip_blocks,
):
    smem = pl.BlockSpec(memory_space=pltpu.SMEM)
    anywhere = pl.BlockSpec(memory_space=pl.ANY)
    vmem = pltpu.VMEM
    dma = pltpu.SemaphoreType.DMA
    return pl.pallas_call(
        kernel,
        out_shape=pltpu.VMEM((COLS, 1024), F32),
        in_specs=[smem] * 3 + [anywhere] * 7,
        out_specs=pl.BlockSpec(memory_space=pltpu.VMEM),
        scratch_shapes=[
            vmem((COLS, 1024), F32),
            vmem((3, 1024), F32),
            vmem((8, 128), jnp.int32),
            vmem((2, LEAF, RANK), F32),
            vmem((2, RANK, RANK), F32),
            vmem((4, RANK, RANK), F32),
            vmem((8, RANK, RANK), F32),
            vmem((1024, 1024), BF16),
            vmem((2, LEAF, RANK), BF16),
            vmem((2, LEAF, RANK), BF16),
            vmem((2, RANK, RANK), BF16),
            vmem((2, RANK, RANK), BF16),
            vmem((4, RANK, RANK), BF16),
            vmem((4, RANK, RANK), BF16),
            vmem((4, RANK, RANK), BF16),
            vmem((4, RANK, RANK), BF16),
            vmem((8, LEAF, LEAF), BF16),
            vmem((8, LEAF, LEAF), BF16),
            vmem((6, LEAF, 128), F32),
            vmem((6, 8, LEAF), F32),
            vmem((6, COLS, LEAF), F32),
            vmem((6, COLS, LEAF), F32),
            vmem((6, COLS, RANK), F32),
            vmem((6, COLS, RANK), F32),
            vmem((2, COLS, RANK), F32),
            vmem((2, COLS, RANK), F32),
            vmem((2, COLS, RANK), F32),
            vmem((2, 4, COLS, RANK), F32),
            vmem((2, COLS, RANK), F32),
            vmem((2, COLS, RANK), F32),
            vmem((2, COLS, LEAF), F32),
            vmem((2, 8, 128), F32),
            vmem((30, 8, 128), F32),
            dma((7,)),
            dma((54,)),
            dma((54,)),
        ],
        compiler_params=pltpu.CompilerParams(
            collective_id=0, has_side_effects=True, vmem_limit_bytes=56 * 1024 * 1024
        ),
    )(
        near_list, far_leaf_list, far_chip_list, probes, points, leaf_order.reshape(8, 128),
        leaf_basis, transfer, far_leaf_blocks, far_chip_blocks,
    )


def solution(mesh):
    both = ("leaf", "sub")
    return jax.shard_map(
        on_device,
        mesh=mesh,
        in_specs=(
            P(None, both), P(None, both), P(both), P(both, None), P(both, None), P("leaf", None),
            P(both, None, None), P(both, None, None), P(both, None, None), P("leaf", None, None),
        ),
        out_specs=P(None, both),
        check_vma=False,
    )
```
